32 devices in a mesh: slab: 8 (over z, x), head: 4 (over y, core).
Axes of the slice: x: 2, y: 2, z: 4, core: 2. Of those that a mesh axis runs over, the one named last changes fastest.
Arguments:
- query_in: bfloat16 [3072, 3072], P(('slab', 'head')), may hold values from -6 to 6
- key_in: bfloat16 [3072, 3072], P(('slab', 'head')), may hold values from -6 to 6
- value_in: bfloat16 [3072, 3072], P(('slab', 'head')), may hold values from -6 to 6
- grad_out: bfloat16 [3072, 3072], P(('slab', 'head')), may hold values from -6 to 6
- neighbours: int32 [48, 16], P('slab'), may hold values from -1 to 47, as said below
Outputs:
- attended: bfloat16 [3072, 3072], P(('slab', 'head'))
- grad_query: bfloat16 [3072, 3072], P(('slab', 'head'))
- grad_key: bfloat16 [3072, 3072], P(('slab', 'head'))
- grad_value: bfloat16 [3072, 3072], P(('slab', 'head'))
The draws below stay inside these ranges and needn't reach their ends.
Inputs may be any that keep to these rules, and one draw needn't show every extreme that they name: `neighbours`: slab s is tiles s * 6 to (s + 1) * 6 - 1. Row t names distinct key tiles, all in the slab of tile t or in the slabs directly before and after it; its first entry is t itself; -1 marks an unused slot, which names no tile.
All inputs are finite; a program needn't handle non-finite values.
Results may differ from the reference program's by a relative error of at most 0.018.
Values may be sent and summed in bfloat16 or wider, within the bound.
No kernel may reach another device: no remote copies, remote signals or barrier semaphores. Data moves between devices by JAX's collectives and lax.ppermute only.
A program may use at most 64 MiB of HBM per device.

```python
import math
import jax
import jax.numpy as jnp
from jax import lax

HEADS = 24
HD = 128
TILE = 64
STILES = 6
NBR = 16
TOKENS = 3072
N_SLAB = 8


def draw_neighbours(key, part):
    tile_total = STILES * N_SLAB
    tile_ids = jnp.arange(tile_total, dtype=jnp.int32)
    slab_of = tile_ids // STILES
    local_pos = tile_ids % STILES
    candidate = jnp.arange(3 * STILES, dtype=jnp.int32)
    key_ids = (slab_of[:, None] - 1) * STILES + candidate[None, :]
    usable = (key_ids >= 0) & (key_ids < tile_total)
    jitter = jax.random.randint(key, (tile_total, 3 * STILES), 0, 1 << 16, dtype=jnp.int32)
    ranking = jitter * 4096 + candidate[None, :]
    same_place = candidate[None, :] % STILES == local_pos[:, None]
    ranking = jnp.where(same_place, (2 << 28) + candidate[None, :], ranking)
    itself = candidate[None, :] == STILES + local_pos[:, None]
    ranking = jnp.where(itself, 3 << 28, ranking)
    ranking = jnp.where(usable, ranking, -1 - candidate[None, :])
    chosen_order = jnp.argsort(-ranking, axis=1, stable=True)[:, :NBR]
    picked = jnp.take_along_axis(key_ids, chosen_order, axis=1)
    picked_ok = jnp.take_along_axis(usable, chosen_order, axis=1)
    return jnp.where(picked_ok, picked, -1).astype(jnp.int32)


def draw_query_in(key, part):
    shape_all = (TOKENS, HEADS * HD)
    values_drawn = jnp.clip(jax.random.normal(jax.random.fold_in(key, 1), shape_all, jnp.float32), -6.0, 6.0)
    return values_drawn.astype(jnp.bfloat16)


def draw_key_in(key, part):
    shape_all = (TOKENS, HEADS * HD)
    values_drawn = jnp.clip(jax.random.normal(jax.random.fold_in(key, 2), shape_all, jnp.float32), -6.0, 6.0)
    return values_drawn.astype(jnp.bfloat16)


def steps_of(rng, shape, cuts, least, largest):
    def one(dim, parts):
        heights = jax.random.uniform(jax.random.fold_in(jax.random.fold_in(rng, 6), dim), (parts,), jnp.float32, least / len(cuts), largest / len(cuts))
        return jnp.repeat(jnp.exp(heights), shape[dim] // parts).reshape((-1,) + (1,) * (len(shape) - dim - 1))

    gain = one(*cuts[0])
    for cut in cuts[1:]:
        gain = gain * one(*cut)
    return gain


def noise(key, dims, deviation, bound, split=(), kind=jnp.bfloat16):
    array = jax.random.normal(key, dims, jnp.float32) * deviation
    if len(split) > 0:
        array = steps_of(key, dims, split, -0.22, 0.18) * array
    return jnp.clip(array, min=-bound, max=bound).astype(kind)


def setup_inputs(seed: int = 0) -> dict:
    arg_keys = jax.random.split(jax.random.key(seed), 6)
    query_in = draw_query_in(jax.random.fold_in(arg_keys[5], 71), 0)
    key_in = draw_key_in(jax.random.fold_in(arg_keys[5], 71), 0)
    value_in = noise(arg_keys[2], (TOKENS, HEADS * HD), 1.0, 6.0, ((0, 32),))
    grad_out = noise(arg_keys[3], (TOKENS, HEADS * HD), 1.0, 6.0, ((0, 32),))
    neighbours = draw_neighbours(jax.random.fold_in(arg_keys[5], 71), 0)
    return {"query_in": query_in, "key_in": key_in, "value_in": value_in, "grad_out": grad_out, "neighbours": neighbours}


def window_mask(id_rows, first_tile, key_count):
    tiles_key = key_count // TILE
    tile_ids = first_tile + jnp.arange(tiles_key, dtype=jnp.int32)
    listed = jnp.any((id_rows[:, :, None] == tile_ids[None, None, :]) & (id_rows[:, :, None] >= 0), axis=1)
    tile_count = id_rows.shape[0]
    spread = jnp.broadcast_to(listed[:, None, :, None], (tile_count, TILE, tiles_key, TILE))
    return spread.reshape(tile_count * TILE, key_count)

def reference(query_in, key_in, value_in, grad_out, neighbours):
    score_scale = 1.0 / math.sqrt(HD)
    full_width = query_in.shape[1]
    head_count = full_width // HD
    slab_rows = STILES * TILE
    zeros_rim = jnp.zeros((slab_rows, full_width), jnp.bfloat16)
    key_pad = jnp.concatenate([zeros_rim, key_in, zeros_rim], axis=0)
    val_pad = jnp.concatenate([zeros_rim, value_in, zeros_rim], axis=0)
    acc_zero = jnp.zeros((key_in.shape[0] + 2 * slab_rows, 2 * full_width), jnp.float32)

    def slab_step(grad_acc, slab_index):
        row_start = (slab_index * slab_rows).astype(jnp.int32)
        query_rows = lax.dynamic_slice_in_dim(query_in, row_start, slab_rows, 0)
        grad_rows = lax.dynamic_slice_in_dim(grad_out, row_start, slab_rows, 0)
        id_rows = lax.dynamic_slice_in_dim(neighbours, (slab_index * STILES).astype(jnp.int32), STILES, 0)
        key_win = lax.dynamic_slice_in_dim(key_pad, row_start, 3 * slab_rows, 0)
        val_win = lax.dynamic_slice_in_dim(val_pad, row_start, 3 * slab_rows, 0)
        first_tile = ((slab_index - 1) * STILES).astype(jnp.int32)
        allowed = window_mask(id_rows, first_tile, 3 * slab_rows)[None]
        query_heads = query_rows.reshape(slab_rows, head_count, HD).astype(jnp.float32)
        grad_heads = grad_rows.reshape(slab_rows, head_count, HD).astype(jnp.float32)
        key_heads = key_win.reshape(3 * slab_rows, head_count, HD).astype(jnp.float32)
        val_heads = val_win.reshape(3 * slab_rows, head_count, HD).astype(jnp.float32)
        scores = jnp.einsum('qhd,khd->hqk', query_heads, key_heads) * score_scale
        scores = jnp.where(allowed, scores, -1e+30)
        row_peak = lax.optimization_barrier(jnp.max(scores, axis=2, keepdims=True))
        log_total = row_peak + jnp.log(lax.optimization_barrier(jnp.sum(jnp.exp(scores - row_peak), axis=2, keepdims=True)))
        weights = jnp.where(allowed, jnp.exp(scores - log_total), 0.0)
        weights_low = weights.astype(jnp.bfloat16).astype(jnp.float32)
        out_heads = jnp.einsum('hqk,khd->qhd', weights_low, val_heads).astype(jnp.bfloat16)
        out_dot = lax.optimization_barrier(jnp.sum(grad_heads * out_heads.astype(jnp.float32), axis=2))
        dweights = jnp.einsum('qhd,khd->hqk', grad_heads, val_heads)
        dscores = (weights * (dweights - out_dot.T[:, :, None])).astype(jnp.bfloat16).astype(jnp.float32)
        dq_heads = (jnp.einsum('hqk,khd->qhd', dscores, key_heads) * score_scale).astype(jnp.bfloat16)
        dk_win = jnp.einsum('hqk,qhd->khd', dscores, query_heads) * score_scale
        dv_win = jnp.einsum('hqk,qhd->khd', weights_low, grad_heads)
        stacked = jnp.concatenate([dk_win.reshape(3 * slab_rows, full_width), dv_win.reshape(3 * slab_rows, full_width)], axis=1)
        current = lax.dynamic_slice_in_dim(grad_acc, row_start, 3 * slab_rows, 0)
        grad_acc = lax.dynamic_update_slice_in_dim(grad_acc, current + stacked, row_start, 0)
        return (grad_acc, (out_heads.reshape(slab_rows, full_width), dq_heads.reshape(slab_rows, full_width)))
    grad_acc, (out_rows, dq_rows) = lax.scan(slab_step, acc_zero, jnp.arange(N_SLAB, dtype=jnp.int32))
    inner = grad_acc[slab_rows:slab_rows + key_in.shape[0]]
    attended = out_rows.reshape(key_in.shape[0], full_width)
    grad_query = dq_rows.reshape(key_in.shape[0], full_width)
    grad_key = inner[:, :full_width].astype(jnp.bfloat16)
    grad_value = inner[:, full_width:].astype(jnp.bfloat16)
    return (attended, grad_query, grad_key, grad_value)
```

```python
import functools
import math

import jax
import jax.numpy as jnp
from jax import lax
from jax.experimental import pallas as pl
from jax.experimental.pallas import tpu as pltpu
from jax.sharding import Mesh
from jax.sharding import PartitionSpec as P

HD = 128
TILE = 64
PAIR = 2
MASKED = -1e30


def window_bias(id_rows, first_tile, key_tiles):
    tile_ids = first_tile + jnp.arange(key_tiles, dtype=jnp.int32)
    listed = jnp.any(
        (id_rows[:, :, None] == tile_ids[None, None, :]) & (id_rows[:, :, None] >= 0), axis=1
    )
    bias = jnp.where(listed, 0.0, MASKED).astype(jnp.float32)
    return jnp.repeat(bias, TILE, axis=1)


def attend_kernel(bias_ref, qg_ref, kv_ref, before_ref, after_ref, oq_ref, own_ref, back_ref, ahead_ref):
    scale = 1.0 / math.sqrt(HD)
    log2_scale = scale * math.log2(math.e)
    blocks, _, rows, _ = qg_ref.shape
    half = blocks // 2
    slab = half * rows
    tiles = slab // TILE

    def flat(ref, low, high, which):
        return ref[low:high, which].reshape((high - low) * rows, HD)

    keys = [flat(before_ref, 0, half, 0), flat(kv_ref, 0, half, 0), flat(kv_ref, half, blocks, 0), flat(after_ref, 0, half, 0)]
    vals = [flat(before_ref, 0, half, 1), flat(kv_ref, 0, half, 1), flat(kv_ref, half, blocks, 1), flat(after_ref, 0, half, 1)]
    key_grads = [None] * 4
    val_grads = [None] * 4
    nt = (((1,), (1,)), ((), ()))
    nn = (((1,), (0,)), ((), ()))
    tn = (((0,), (0,)), ((), ()))
    dot = functools.partial(lax.dot_general, preferred_element_type=jnp.float32)
    for part in range(2):
        query = flat(qg_ref, part * half, (part + 1) * half, 0)
        grad = flat(qg_ref, part * half, (part + 1) * half, 1)
        key_win = jnp.concatenate(keys[part : part + 3], axis=0)
        val_win = jnp.concatenate(vals[part : part + 3], axis=0)
        bias = bias_ref[part * tiles : (part + 1) * tiles]
        bias = jnp.broadcast_to(bias[:, None, :], (tiles, TILE, bias.shape[1])).reshape(slab, bias.shape[1])
        scores = dot(query, key_win, nt) + bias
        peak = jnp.max(scores, axis=1, keepdims=True)
        weights = jnp.exp2((scores - peak) * log2_scale)
        weights = weights * (1.0 / jnp.sum(weights, axis=1, keepdims=True))
        weights_low = weights.astype(jnp.bfloat16)
        out = dot(weights_low, val_win, nn).astype(jnp.bfloat16)
        out_dot = jnp.sum(grad.astype(jnp.float32) * out.astype(jnp.float32), axis=1, keepdims=True)
        dweights = dot(grad, val_win, nt)
        dscores = (weights * (dweights - out_dot)).astype(jnp.bfloat16)
        dquery = (dot(dscores, key_win, nn) * scale).astype(jnp.bfloat16)
        oq_ref[part * half : (part + 1) * half, 0] = out.reshape(half, rows, HD)
        oq_ref[part * half : (part + 1) * half, 1] = dquery.reshape(half, rows, HD)
        dkey = dot(dscores, query, tn) * scale
        dval = dot(weights_low, grad, tn)
        for third in range(3):
            at = part + third
            dk = dkey[third * slab : (third + 1) * slab]
            dv = dval[third * slab : (third + 1) * slab]
            key_grads[at] = dk if key_grads[at] is None else key_grads[at] + dk
            val_grads[at] = dv if val_grads[at] is None else val_grads[at] + dv
    for which, grads in enumerate((key_grads, val_grads)):
        back_ref[:, which] = grads[0].reshape(half, rows, HD).astype(jnp.bfloat16)
        own_ref[:half, which] = grads[1].reshape(half, rows, HD)
        own_ref[half:, which] = grads[2].reshape(half, rows, HD)
        ahead_ref[:, which] = grads[3].reshape(half, rows, HD).astype(jnp.bfloat16)


def attend(bias, qg, kv, before, after):
    blocks, _, rows, width = qg.shape
    half = blocks // 2

    def spec(count):
        return pl.BlockSpec((count, 2, rows, HD), lambda h: (0, 0, 0, h))

    def shape(count, dtype):
        return jax.ShapeDtypeStruct((count, 2, rows, width), dtype)

    pairs = bias.shape[0] * TILE * bias.shape[1] * (width // HD)
    return pl.pallas_call(
        attend_kernel,
        grid=(width // HD,),
        in_specs=[pl.BlockSpec(bias.shape, lambda h: (0, 0)), spec(blocks), spec(blocks), spec(half), spec(half)],
        out_specs=[spec(blocks), spec(blocks), spec(half), spec(half)],
        out_shape=[shape(blocks, jnp.bfloat16), shape(blocks, jnp.float32), shape(half, jnp.bfloat16), shape(half, jnp.bfloat16)],
        compiler_params=pltpu.CompilerParams(vmem_limit_bytes=48 * 1024 * 1024),
        cost_estimate=pl.CostEstimate(flops=12 * pairs * HD, bytes_accessed=16 * 2**20, transcendentals=pairs),
    )(bias, qg, kv, before, after)


def per_device(query_in, key_in, value_in, grad_out, neighbours):
    plane = ("pair", "head")
    peers = lax.axis_size(plane)
    groups = lax.axis_size("group")
    rows, full_width = query_in.shape
    slab_tiles = neighbours.shape[0]
    half = peers // PAIR

    def outgoing(first, second):
        joined = jnp.stack([first.reshape(rows, peers, -1), second.reshape(rows, peers, -1)], axis=0)
        return jnp.transpose(joined, (2, 0, 1, 3))

    def incoming(joined):
        first, second = joined[:, 0], joined[:, 1]
        return (
            jnp.transpose(first, (1, 0, 2)).reshape(rows, full_width),
            jnp.transpose(second, (1, 0, 2)).reshape(rows, full_width),
        )

    up = [(i, i + 1) for i in range(groups - 1)]
    down = [(i + 1, i) for i in range(groups - 1)]
    slab = lax.axis_index("group") * PAIR + lax.axis_index("pair")
    bias = window_bias(neighbours, (slab - 1) * slab_tiles, 3 * slab_tiles)
    other = lax.ppermute(bias, "pair", [(0, 1), (1, 0)])
    first = lax.axis_index("pair") == 0
    bias = jnp.concatenate([jnp.where(first, bias, other), jnp.where(first, other, bias)], axis=0)
    kv = lax.all_to_all(outgoing(key_in, value_in), plane, 0, 0, tiled=True)
    before = lax.ppermute(kv[half:], "group", up)
    after = lax.ppermute(kv[:half], "group", down)
    qg = lax.all_to_all(outgoing(query_in, grad_out), plane, 0, 0, tiled=True)
    oq, own, back, ahead = attend(bias, qg, kv, before, after)
    from_before = lax.ppermute(ahead, "group", up)
    from_after = lax.ppermute(back, "group", down)
    attended, grad_query = incoming(lax.all_to_all(oq, plane, 0, 0, tiled=True))
    arrived = jnp.concatenate([from_before, from_after], axis=0).astype(jnp.float32)
    grads = (own + arrived).astype(jnp.bfloat16)
    grad_key, grad_value = incoming(lax.all_to_all(grads, plane, 0, 0, tiled=True))
    return attended, grad_query, grad_key, grad_value


def solution(mesh):
    slabs, heads = mesh.devices.shape
    paired = Mesh(mesh.devices.reshape(slabs // PAIR, PAIR, heads), ("group", "pair", "head"))
    tokens = P(("group", "pair", "head"), None)
    return jax.shard_map(
        per_device,
        mesh=paired,
        in_specs=(tokens, tokens, tokens, tokens, P(("group", "pair"), None)),
        out_specs=(tokens, tokens, tokens, tokens),
        check_vma=False,
    )
```

```python
import functools
import math

import jax
import jax.numpy as jnp
from jax import lax
from jax.experimental import pallas as pl
from jax.experimental.pallas import tpu as pltpu
from jax.sharding import Mesh
from jax.sharding import PartitionSpec as P

HD = 128
TILE = 64
MASKED = -1e30
AXES = ("group", "pair", "row", "core")
PLANE = ("pair", "row", "core")
SHIFTS = ((1, 1), (0, 0), (0, 1), (1, 0))
CHUNKS = 3
ANY = pl.BlockSpec(memory_space=pl.ANY)
BF16 = jnp.bfloat16


def head_group(shift):
    a, b = shift
    rows = lax.axis_size("row")
    return (lax.axis_index("core") ^ a) * rows + lax.rem(lax.axis_index("row") + b, rows)


def run_copies(copies):
    for copy in copies:
        copy.start()
    for copy in copies:
        copy.wait()


def pack_kernel(offset, width, group_width, *refs):
    arrays, messages, sem = refs[:4], refs[4:8], refs[8]
    copies = []
    for i, shift in enumerate(SHIFTS):
        column = pl.multiple_of(head_group(shift) * group_width + offset, HD)
        for j, array in enumerate(arrays):
            copies.append(
                pltpu.make_async_copy(array.at[:, pl.ds(column, width)], messages[i].at[j], sem.at[i, j])
            )
    run_copies(copies)


def pack(arrays, offset, width, group_width):
    rows = arrays[0].shape[0]
    return pl.pallas_call(
        functools.partial(pack_kernel, offset, width, group_width),
        in_specs=[ANY] * 4,
        out_specs=[ANY] * 4,
        out_shape=[jax.ShapeDtypeStruct((4, rows, width), BF16)] * 4,
        scratch_shapes=[pltpu.SemaphoreType.DMA((4, 4))],
        cost_estimate=pl.CostEstimate(flops=0, bytes_accessed=32 * rows * width * 2, transcendentals=0),
    )(*arrays)


def unpack_kernel(offset, width, group_width, *refs):
    messages, sem = refs[:4], refs[-1]
    arrays = refs[-3:-1]
    copies = []
    for i, shift in enumerate(SHIFTS):
        column = pl.multiple_of(head_group(shift) * group_width + offset, HD)
        for j, array in enumerate(arrays):
            copies.append(
                pltpu.make_async_copy(messages[i].at[j], array.at[:, pl.ds(column, width)], sem.at[i, j])
            )
    run_copies(copies)


def unpack(messages, arrays, offset, group_width, full_width):
    _, rows, width = messages[0].shape
    held = [] if arrays is None else list(arrays)
    return pl.pallas_call(
        functools.partial(unpack_kernel, offset, width, group_width),
        in_specs=[ANY] * (4 + len(held)),
        out_specs=[ANY] * 2,
        out_shape=[jax.ShapeDtypeStruct((rows, full_width), BF16)] * 2,
        input_output_aliases={4 + i: i for i in range(len(held))},
        scratch_shapes=[pltpu.SemaphoreType.DMA((4, 2))],
        cost_estimate=pl.CostEstimate(flops=0, bytes_accessed=16 * rows * width * 2, transcendentals=0),
    )(*messages, *held)


def join_kernel(*refs):
    messages, joined, sem = refs[:4], refs[4], refs[5]
    run_copies([pltpu.make_async_copy(m.at[:2], joined.at[i], sem.at[i]) for i, m in enumerate(messages)])


def join(messages):
    _, rows, width = messages[0].shape
    return pl.pallas_call(
        join_kernel,
        in_specs=[ANY] * 4,
        out_specs=ANY,
        out_shape=jax.ShapeDtypeStruct((4, 2, rows, width), BF16),
        scratch_shapes=[pltpu.SemaphoreType.DMA((4,))],
        cost_estimate=pl.CostEstimate(flops=0, bytes_accessed=16 * rows * width * 2, transcendentals=0),
    )(*messages)


def attend_kernel(bias_ref, *refs):
    messages, other_ref, halo_ref = refs[:4], refs[4], refs[5]
    oq_refs, own_out, other_out, halo_out = refs[6:10], refs[10], refs[11], refs[12]
    scale = 1.0 / math.sqrt(HD)
    log2_scale = scale * math.log2(math.e)
    rows = other_ref.shape[2]
    slab = 4 * rows

    def window(which):
        return jnp.concatenate(
            [m[which] for m in messages]
            + [other_ref[:, which].reshape(slab, HD), halo_ref[:, which].reshape(slab, HD)],
            axis=0,
        )

    nt = (((1,), (1,)), ((), ()))
    nn = (((1,), (0,)), ((), ()))
    tn = (((0,), (0,)), ((), ()))
    dot = functools.partial(lax.dot_general, preferred_element_type=jnp.float32)
    key_win, val_win = window(0), window(1)
    query = jnp.concatenate([m[2] for m in messages], axis=0)
    grad = jnp.concatenate([m[3] for m in messages], axis=0)
    scores = dot(query, key_win, nt) + bias_ref[...]
    peak = jnp.max(scores, axis=1, keepdims=True)
    weights = jnp.exp2((scores - peak) * log2_scale)
    weights = weights * (1.0 / jnp.sum(weights, axis=1, keepdims=True))
    weights_low = weights.astype(BF16)
    out = dot(weights_low, val_win, nn).astype(BF16)
    out_dot = jnp.sum(grad.astype(jnp.float32) * out.astype(jnp.float32), axis=1, keepdims=True)
    dweights = dot(grad, val_win, nt)
    dscores = (weights * (dweights - out_dot)).astype(BF16)
    dquery = (dot(dscores, key_win, nn) * scale).astype(BF16)
    for i, ref in enumerate(oq_refs):
        ref[0] = out[i * rows : (i + 1) * rows]
        ref[1] = dquery[i * rows : (i + 1) * rows]
    grads = (dot(dscores, query, tn) * scale, dot(weights_low, grad, tn))
    for which, value in enumerate(grads):
        for third, ref in enumerate((own_out, other_out, halo_out)):
            piece = value[third * slab : (third + 1) * slab]
            ref[:, which] = piece.reshape(4, rows, HD).astype(ref.dtype)


def attend(bias, messages, other, halo):
    _, rows, width = messages[0].shape
    heads = width // HD
    four = pl.BlockSpec((4, rows, HD), lambda h: (0, 0, h))
    two = pl.BlockSpec((2, rows, HD), lambda h: (0, 0, h))
    joined = pl.BlockSpec((4, 2, rows, HD), lambda h: (0, 0, 0, h))
    pairs = bias.shape[0] * bias.shape[1] * heads
    shapes = [jax.ShapeDtypeStruct((2, rows, width), BF16)] * 4
    shapes += [jax.ShapeDtypeStruct((4, 2, rows, width), t) for t in (jnp.float32, BF16, BF16)]
    outs = pl.pallas_call(
        attend_kernel,
        grid=(heads,),
        in_specs=[pl.BlockSpec(bias.shape, lambda h: (0, 0))] + [four] * 4 + [joined] * 2,
        out_specs=[two] * 4 + [joined] * 3,
        out_shape=shapes,
        compiler_params=pltpu.CompilerParams(vmem_limit_bytes=40 * 1024 * 1024),
        cost_estimate=pl.CostEstimate(flops=12 * pairs * HD, bytes_accessed=6 * 2**20, transcendentals=pairs),
    )(bias, *messages, other, halo)
    return outs[:4], outs[4], outs[5], outs[6]


def total_kernel(own_ref, other_ref, halo_ref, *outs):
    for i, ref in enumerate(outs):
        total = own_ref[i] + other_ref[i].astype(jnp.float32) + halo_ref[i].astype(jnp.float32)
        ref[...] = total.astype(BF16)


def total(own, other, halo):
    _, _, rows, width = own.shape
    joined = pl.BlockSpec((4, 1, rows, width), lambda k: (0, k, 0, 0))
    return pl.pallas_call(
        total_kernel,
        grid=(2,),
        in_specs=[joined] * 3,
        out_specs=[pl.BlockSpec((1, rows, width), lambda k: (k, 0, 0))] * 4,
        out_shape=[jax.ShapeDtypeStruct((2, rows, width), BF16)] * 4,
        cost_estimate=pl.CostEstimate(flops=own.size * 2, bytes_accessed=own.size * 10, transcendentals=0),
    )(own, other, halo)


def window_bias(neighbours, rows):
    tiles = neighbours.shape[0]
    slab_rows = tiles * TILE
    core = lax.axis_index("core")
    swap = []
    sizes = [lax.axis_size(a) for a in PLANE]
    index = lambda p, r, c: (p * sizes[1] + r) * 2 + c
    for p in range(2):
        for r in range(sizes[1]):
            for c in range(2):
                swap.append((index(p, r, c), index(c, r, p)))
    ids = lax.ppermute(neighbours, PLANE, swap)
    slab = lax.axis_index("group") * 2 + core
    window_ids = (slab - 1) * tiles + jnp.arange(3 * tiles, dtype=jnp.int32)
    listed = jnp.any((ids[:, :, None] == window_ids[None, None, :]) & (ids[:, :, None] >= 0), axis=1)
    blocks = []
    for a, b in SHIFTS:
        source_row = lax.rem(lax.axis_index("row") - b + sizes[1], sizes[1])
        blocks.append(source_row * 2 + (lax.axis_index("pair") ^ a))
    token = (jnp.stack(blocks)[:, None] * rows + jnp.arange(rows, dtype=jnp.int32)[None, :]).reshape(slab_rows)
    tile = token // TILE
    other = jnp.where(core == 0, 2 * tiles, 0)
    columns = jnp.concatenate([tile + tiles, tile + other, tile + 2 * tiles - other])
    pick_rows = (tile[:, None] == jnp.arange(tiles)[None, :]).astype(BF16)
    pick_columns = (jnp.arange(3 * tiles)[:, None] == columns[None, :]).astype(BF16)
    spread = jnp.dot(listed.astype(BF16), pick_columns)
    allowed = jnp.dot(pick_rows, spread, preferred_element_type=jnp.float32)
    return jnp.where(allowed > 0.5, 0.0, MASKED).astype(jnp.float32)


def per_device(query_in, key_in, value_in, grad_out, neighbours):
    groups, rings = lax.axis_size("group"), lax.axis_size("row")
    rows, full_width = query_in.shape
    group_width = full_width // (2 * rings)
    width = group_width // CHUNKS

    def place(g, p, r, c):
        return ((g * 2 + p) * rings + r) * 2 + c

    everyone = [(g, p, r, c) for g in range(groups) for p in range(2) for r in range(rings) for c in range(2)]

    def spread_pairs(shift):
        a, b = shift
        return [(place(g, p, r, c), place(g, c ^ a, (r + b) % rings, p)) for g, p, r, c in everyone]

    beside = []
    for g, p, r, c in everyone:
        to = g + 1 if c == 1 else g - 1
        if 0 <= to < groups:
            beside.append((place(g, p, r, c), place(to, p, r, 1 - c)))

    def send(messages):
        return [lax.ppermute(m, AXES, spread_pairs(s)) for m, s in zip(messages, SHIFTS)]

    def send_back(messages):
        return [
            lax.ppermute(m, AXES, [(d, s) for s, d in spread_pairs(shift)]) for m, shift in zip(messages, SHIFTS)
        ]

    def across(x):
        return lax.ppermute(x, "core", [(0, 1), (1, 0)])

    def halo(x):
        return lax.ppermute(x, AXES, beside)

    bias = window_bias(neighbours, rows)
    arrays = (key_in, value_in, query_in, grad_out)
    offsets = [k * width for k in range(CHUNKS)]
    received = [send(pack(arrays, offset, width, group_width)) for offset in offsets]
    forward = backward = None
    for k, offset in enumerate(offsets):
        messages = received[k]
        joined = join(messages)
        oq, own, other, far = attend(bias, messages, across(joined), halo(joined))
        grads = total(own, across(other), halo(far))
        forward = unpack(send_back(oq), forward, offset, group_width, full_width)
        backward = unpack(send_back(grads), backward, offset, group_width, full_width)
    return forward[0], forward[1], backward[0], backward[1]


def solution(mesh):
    slabs, heads = mesh.devices.shape
    paired = Mesh(mesh.devices.reshape(slabs // 2, 2, heads // 2, 2), AXES)
    tokens = P(AXES, None)
    return jax.shard_map(
        per_device,
        mesh=paired,
        in_specs=(tokens, tokens, tokens, tokens, P(("group", "pair"), None)),
        out_specs=(tokens, tokens, tokens, tokens),
        check_vma=False,
    )
```

```python
import functools
import math

import jax
import jax.numpy as jnp
from jax import lax
from jax.experimental import pallas as pl
from jax.experimental.pallas import tpu as pltpu
from jax.sharding import Mesh
from jax.sharding import PartitionSpec as P

HD = 128
TILE = 64
MASKED = -1e30
AXES = ("group", "pair", "row", "core")
PLANE = ("pair", "row", "core")
SHIFTS = ((1, 1), (0, 0), (0, 1), (1, 0))
BF16 = jnp.bfloat16
ANY = pl.BlockSpec(memory_space=pl.ANY)


def head_group(shift):
    a, b = shift
    rows = lax.axis_size("row")
    return (lax.axis_index("core") ^ a) * rows + lax.rem(lax.axis_index("row") + b, rows)


MIB = 1024 * 1024


def limit(mib):
    return pltpu.CompilerParams(vmem_limit_bytes=mib * MIB)


def pack_kernel(first, second, *refs):
    messages, held, loads, stores = refs[:4], refs[4], refs[5], refs[6]
    width = held.shape[3]
    ins, outs = [], []
    for i, message in enumerate(messages):
        columns = pl.ds(pl.multiple_of(head_group(SHIFTS[i]) * width, HD), width)
        ins.append([pltpu.make_async_copy(a.at[:, columns], held.at[i, j], loads.at[i, j]) for j, a in enumerate((first, second))])
        outs.append(pltpu.make_async_copy(held.at[i], message, stores.at[i]))
    for pair in ins:
        for copy in pair:
            copy.start()
    for pair, out in zip(ins, outs):
        for copy in pair:
            copy.wait()
        out.start()
    for out in outs:
        out.wait()


def pack(first, second, group_width):
    rows = first.shape[0]
    return pl.pallas_call(
        pack_kernel,
        in_specs=[ANY, ANY],
        out_specs=[ANY] * 4,
        out_shape=[jax.ShapeDtypeStruct((2, rows, group_width), BF16)] * 4,
        scratch_shapes=[
            pltpu.VMEM((4, 2, rows, group_width), BF16),
            pltpu.SemaphoreType.DMA((4, 2)),
            pltpu.SemaphoreType.DMA((4,)),
        ],
        compiler_params=limit(60),
        cost_estimate=pl.CostEstimate(flops=0, bytes_accessed=32 * rows * group_width, transcendentals=0),
    )(first, second)


def unpack_kernel(*refs):
    messages, arrays, held, loads, stores = refs[:4], refs[4:6], refs[6], refs[7], refs[8]
    width = held.shape[3]
    ins, outs = [], []
    for i, message in enumerate(messages):
        columns = pl.ds(pl.multiple_of(head_group(SHIFTS[i]) * width, HD), width)
        ins.append(pltpu.make_async_copy(message, held.at[i], loads.at[i]))
        outs.append([pltpu.make_async_copy(held.at[i, j], a.at[:, columns], stores.at[i, j]) for j, a in enumerate(arrays)])
    for copy in ins:
        copy.start()
    for copy, pair in zip(ins, outs):
        copy.wait()
        for out in pair:
            out.start()
    for pair in outs:
        for out in pair:
            out.wait()


def unpack(messages, full_width):
    _, rows, width = messages[0].shape
    return pl.pallas_call(
        unpack_kernel,
        in_specs=[ANY] * 4,
        out_specs=[ANY] * 2,
        out_shape=[jax.ShapeDtypeStruct((rows, full_width), BF16)] * 2,
        scratch_shapes=[
            pltpu.VMEM((4, 2, rows, width), BF16),
            pltpu.SemaphoreType.DMA((4,)),
            pltpu.SemaphoreType.DMA((4, 2)),
        ],
        compiler_params=limit(4),
        cost_estimate=pl.CostEstimate(flops=0, bytes_accessed=8 * rows * full_width, transcendentals=0),
    )(*messages)


def join_kernel(*refs):
    messages, joined, held, loads, stores = refs[:4], refs[4], refs[5], refs[6], refs[7]
    ins = [pltpu.make_async_copy(m, held.at[i], loads.at[i]) for i, m in enumerate(messages)]
    outs = [pltpu.make_async_copy(held.at[i], joined.at[i], stores.at[i]) for i in range(4)]
    for copy in ins:
        copy.start()
    for copy, out in zip(ins, outs):
        copy.wait()
        out.start()
    for out in outs:
        out.wait()


def join(messages):
    _, rows, width = messages[0].shape
    return pl.pallas_call(
        join_kernel,
        in_specs=[ANY] * 4,
        out_specs=ANY,
        out_shape=jax.ShapeDtypeStruct((4, 2, rows, width), BF16),
        scratch_shapes=[
            pltpu.VMEM((4, 2, rows, width), BF16),
            pltpu.SemaphoreType.DMA((4,)),
            pltpu.SemaphoreType.DMA((4,)),
        ],
        compiler_params=limit(4),
        cost_estimate=pl.CostEstimate(flops=0, bytes_accessed=32 * rows * width, transcendentals=0),
    )(*messages)


def attend_kernel(bias_ref, *refs):
    queries, own_ref, other_ref, halo_ref = refs[:4], refs[4], refs[5], refs[6]
    oq_refs, own_out, other_out, halo_out = refs[7:11], refs[11], refs[12], refs[13]
    scale = 1.0 / math.sqrt(HD)
    log2_scale = scale * math.log2(math.e)
    rows = other_ref.shape[2]
    slab = 4 * rows

    def window(which):
        return jnp.concatenate([ref[:, which].reshape(slab, HD) for ref in (own_ref, other_ref, halo_ref)], axis=0)

    nt = (((1,), (1,)), ((), ()))
    nn = (((1,), (0,)), ((), ()))
    tn = (((0,), (0,)), ((), ()))
    dot = functools.partial(lax.dot_general, preferred_element_type=jnp.float32)
    key_win, val_win = window(0), window(1)
    query = jnp.concatenate([m[0] for m in queries], axis=0)
    grad = jnp.concatenate([m[1] for m in queries], axis=0)
    scores = dot(query, key_win, nt) + bias_ref[...]
    peak = jnp.max(scores, axis=1, keepdims=True)
    weights = jnp.exp2((scores - peak) * log2_scale)
    weights = weights * (1.0 / jnp.sum(weights, axis=1, keepdims=True))
    weights_low = weights.astype(BF16)
    out = dot(weights_low, val_win, nn).astype(BF16)
    out_dot = jnp.sum(grad.astype(jnp.float32) * out.astype(jnp.float32), axis=1, keepdims=True)
    dweights = dot(grad, val_win, nt)
    dscores = (weights * (dweights - out_dot)).astype(BF16)
    dquery = (dot(dscores, key_win, nn) * scale).astype(BF16)
    for i, ref in enumerate(oq_refs):
        ref[0] = out[i * rows : (i + 1) * rows]
        ref[1] = dquery[i * rows : (i + 1) * rows]
    grads = (dot(dscores, query, tn) * scale, dot(weights_low, grad, tn))
    for which, value in enumerate(grads):
        for third, ref in enumerate((own_out, other_out, halo_out)):
            piece = value[third * slab : (third + 1) * slab]
            ref[:, which] = piece.reshape(4, rows, HD).astype(ref.dtype)


def attend(bias, queries, own, other, halo):
    _, rows, width = queries[0].shape
    heads = width // HD
    two = pl.BlockSpec((2, rows, HD), lambda h: (0, 0, h))
    joined = pl.BlockSpec((4, 2, rows, HD), lambda h: (0, 0, 0, h))
    pairs = bias.shape[0] * bias.shape[1] * heads
    shapes = [jax.ShapeDtypeStruct((2, rows, width), BF16)] * 4
    shapes += [jax.ShapeDtypeStruct((4, 2, rows, width), t) for t in (BF16, BF16, BF16)]
    outs = pl.pallas_call(
        attend_kernel,
        grid=(heads,),
        in_specs=[pl.BlockSpec(bias.shape, lambda h: (0, 0))] + [two] * 4 + [joined] * 3,
        out_specs=[two] * 4 + [joined] * 3,
        out_shape=shapes,
        compiler_params=limit(20),
        cost_estimate=pl.CostEstimate(flops=12 * pairs * HD, bytes_accessed=16 * 2**20, transcendentals=pairs),
    )(bias, *queries, own, other, halo)
    return list(outs[:4]), outs[4], outs[5], outs[6]


def total_kernel(own_ref, other_ref, halo_ref, *outs):
    for i, ref in enumerate(outs):
        total = own_ref[i].astype(jnp.float32) + other_ref[i].astype(jnp.float32) + halo_ref[i].astype(jnp.float32)
        ref[...] = total.astype(BF16)


def total(own, other, halo):
    _, _, rows, width = own.shape
    piece = HD * 2
    joined = pl.BlockSpec((4, 2, rows, piece), lambda k: (0, 0, 0, k))
    return pl.pallas_call(
        total_kernel,
        grid=(width // piece,),
        in_specs=[joined] * 3,
        out_specs=[pl.BlockSpec((2, rows, piece), lambda k: (0, 0, k))] * 4,
        out_shape=[jax.ShapeDtypeStruct((2, rows, width), BF16)] * 4,
        compiler_params=limit(8),
        cost_estimate=pl.CostEstimate(flops=own.size * 2, bytes_accessed=own.size * 10, transcendentals=0),
    )(own, other, halo)


def window_bias(neighbours, rows):
    tiles = neighbours.shape[0]
    slab_rows = tiles * TILE
    core = lax.axis_index("core")
    rings = lax.axis_size("row")
    swap = []
    for p in range(2):
        for r in range(rings):
            for c in range(2):
                swap.append(((p * rings + r) * 2 + c, (c * rings + r) * 2 + p))
    ids = lax.ppermute(neighbours, PLANE, swap)
    slab = lax.axis_index("group") * 2 + core
    window_ids = (slab - 1) * tiles + jnp.arange(3 * tiles, dtype=jnp.int32)
    listed = jnp.any((ids[:, :, None] == window_ids[None, None, :]) & (ids[:, :, None] >= 0), axis=1)
    blocks = []
    for a, b in SHIFTS:
        source_row = lax.rem(lax.axis_index("row") - b + rings, rings)
        blocks.append(source_row * 2 + (lax.axis_index("pair") ^ a))
    token = (jnp.stack(blocks)[:, None] * rows + jnp.arange(rows, dtype=jnp.int32)[None, :]).reshape(slab_rows)
    tile = token // TILE
    other = jnp.where(core == 0, 2 * tiles, 0)
    columns = jnp.concatenate([tile + tiles, tile + other, tile + 2 * tiles - other])
    pick_rows = (tile[:, None] == jnp.arange(tiles)[None, :]).astype(BF16)
    pick_columns = (jnp.arange(3 * tiles)[:, None] == columns[None, :]).astype(BF16)
    spread = jnp.dot(listed.astype(BF16), pick_columns)
    allowed = jnp.dot(pick_rows, spread, preferred_element_type=jnp.float32)
    return jnp.where(allowed > 0.5, 0.0, MASKED).astype(jnp.float32)


def per_device(query_in, key_in, value_in, grad_out, neighbours):
    groups, rings = lax.axis_size("group"), lax.axis_size("row")
    rows, full_width = query_in.shape
    group_width = full_width // (2 * rings)

    def place(g, p, r, c):
        return ((g * 2 + p) * rings + r) * 2 + c

    everyone = [(g, p, r, c) for g in range(groups) for p in range(2) for r in range(rings) for c in range(2)]

    def spread_pairs(shift):
        a, b = shift
        return [(place(g, p, r, c), place(g, c ^ a, (r + b) % rings, p)) for g, p, r, c in everyone]

    beside = []
    for g, p, r, c in everyone:
        to = g + 1 if c == 1 else g - 1
        if 0 <= to < groups:
            beside.append((place(g, p, r, c), place(to, p, r, 1 - c)))

    def send(messages):
        return [lax.ppermute(m, AXES, spread_pairs(s)) for m, s in zip(messages, SHIFTS)]

    def send_back(messages):
        return [
            lax.ppermute(m, AXES, [(d, s) for s, d in spread_pairs(shift)]) for m, shift in zip(messages, SHIFTS)
        ]

    def across(x):
        return lax.ppermute(x, "core", [(0, 1), (1, 0)])

    def halo(x):
        return lax.ppermute(x, AXES, beside)

    key_out = pack(key_in, value_in, group_width)
    key_out, query_in, neighbours = lax.optimization_barrier((key_out, query_in, neighbours))
    query_out = pack(query_in, grad_out, group_width)
    bias = window_bias(neighbours, rows)
    own = join(send(key_out))
    query_out, own = lax.optimization_barrier((query_out, own))
    query_out = list(query_out)
    other = across(own)
    other, query_out[3] = lax.optimization_barrier((other, query_out[3]))
    far = halo(own)
    queries = send(query_out)
    oq, own_part, other_part, far_part = attend(bias, queries, own, other, far)
    other_part = across(other_part)
    other_part, oq[3] = lax.optimization_barrier((other_part, oq[3]))
    grads = total(own_part, other_part, halo(far_part))
    forward = unpack(send_back(oq), full_width)
    return *forward, *unpack(send_back(grads), full_width)


def solution(mesh):
    slabs, heads = mesh.devices.shape
    paired = Mesh(mesh.devices.reshape(slabs // 2, 2, heads // 2, 2), AXES)
    tokens = P(AXES, None)
    return jax.shard_map(
        per_device,
        mesh=paired,
        in_specs=(tokens, tokens, tokens, tokens, P(("group", "pair"), None)),
        out_specs=(tokens, tokens, tokens, tokens),
        check_vma=False,
    )
```

```python
import functools
import math

import jax
import jax.numpy as jnp
from jax import lax
from jax.experimental import pallas as pl
from jax.experimental.pallas import tpu as pltpu
from jax.sharding import Mesh
from jax.sharding import PartitionSpec as P

HD = 128
TILE = 64
EARLY = 1
ABREAST = 2
MASKED = -1e30
AXES = ("group", "pair", "row", "core")
PLANE = ("pair", "row", "core")
SHIFTS = ((1, 1), (0, 0), (0, 1), (1, 0))
BF16 = jnp.bfloat16
ANY = pl.BlockSpec(memory_space=pl.ANY)


def head_group(shift):
    a, b = shift
    rows = lax.axis_size("row")
    return (lax.axis_index("core") ^ a) * rows + lax.rem(lax.axis_index("row") + b, rows)


MIB = 1024 * 1024


def limit(mib):
    return pltpu.CompilerParams(vmem_limit_bytes=mib * MIB)


def pack_kernel(first, second, *refs):
    messages, held, loads, stores = refs[:4], refs[4], refs[5], refs[6]
    width = held.shape[3]
    ins, outs = [], []
    for i, message in enumerate(messages):
        columns = pl.ds(pl.multiple_of(head_group(SHIFTS[i]) * width, HD), width)
        ins.append([pltpu.make_async_copy(a.at[:, columns], held.at[i, j], loads.at[i, j]) for j, a in enumerate((first, second))])
        outs.append(pltpu.make_async_copy(held.at[i], message, stores.at[i]))
    for pair in ins:
        for copy in pair:
            copy.start()
    for pair, out in zip(ins, outs):
        for copy in pair:
            copy.wait()
        out.start()
    for out in outs:
        out.wait()


def pack(first, second, group_width):
    rows = first.shape[0]
    return pl.pallas_call(
        pack_kernel,
        in_specs=[ANY, ANY],
        out_specs=[ANY] * 4,
        out_shape=[jax.ShapeDtypeStruct((2, rows, group_width), BF16)] * 4,
        scratch_shapes=[
            pltpu.VMEM((4, 2, rows, group_width), BF16),
            pltpu.SemaphoreType.DMA((4, 2)),
            pltpu.SemaphoreType.DMA((4,)),
        ],
        compiler_params=limit(60),
        cost_estimate=pl.CostEstimate(flops=0, bytes_accessed=32 * rows * group_width, transcendentals=0),
    )(first, second)


def unpack_kernel(*refs):
    messages, arrays, held, loads, stores = refs[:4], refs[4:6], refs[6], refs[7], refs[8]
    width = held.shape[3]
    ins, outs = [], []
    for i, message in enumerate(messages):
        columns = pl.ds(pl.multiple_of(head_group(SHIFTS[i]) * width, HD), width)
        ins.append(pltpu.make_async_copy(message, held.at[i], loads.at[i]))
        outs.append([pltpu.make_async_copy(held.at[i, j], a.at[:, columns], stores.at[i, j]) for j, a in enumerate(arrays)])
    for copy in ins:
        copy.start()
    for copy, pair in zip(ins, outs):
        copy.wait()
        for out in pair:
            out.start()
    for pair in outs:
        for out in pair:
            out.wait()


def unpack(messages, full_width):
    _, rows, width = messages[0].shape
    return pl.pallas_call(
        unpack_kernel,
        in_specs=[ANY] * 4,
        out_specs=[ANY] * 2,
        out_shape=[jax.ShapeDtypeStruct((rows, full_width), BF16)] * 2,
        scratch_shapes=[
            pltpu.VMEM((4, 2, rows, width), BF16),
            pltpu.SemaphoreType.DMA((4,)),
            pltpu.SemaphoreType.DMA((4, 2)),
        ],
        compiler_params=limit(4),
        cost_estimate=pl.CostEstimate(flops=0, bytes_accessed=8 * rows * full_width, transcendentals=0),
    )(*messages)


def join_kernel(*refs):
    messages, joined, held, loads, stores = refs[:4], refs[4], refs[5], refs[6], refs[7]
    ins = [pltpu.make_async_copy(m, held.at[i], loads.at[i]) for i, m in enumerate(messages)]
    outs = [pltpu.make_async_copy(held.at[i], joined.at[i], stores.at[i]) for i in range(4)]
    for copy in ins:
        copy.start()
    for copy, out in zip(ins, outs):
        copy.wait()
        out.start()
    for out in outs:
        out.wait()


def join(messages):
    _, rows, width = messages[0].shape
    return pl.pallas_call(
        join_kernel,
        in_specs=[ANY] * 4,
        out_specs=ANY,
        out_shape=jax.ShapeDtypeStruct((4, 2, rows, width), BF16),
        scratch_shapes=[
            pltpu.VMEM((4, 2, rows, width), BF16),
            pltpu.SemaphoreType.DMA((4,)),
            pltpu.SemaphoreType.DMA((4,)),
        ],
        compiler_params=limit(4),
        cost_estimate=pl.CostEstimate(flops=0, bytes_accessed=32 * rows * width, transcendentals=0),
    )(*messages)


def attend_kernel(bias_ref, *refs):
    queries, windows = refs[:4], refs[4:7]
    oq_refs, grad_refs = refs[7:11], refs[11:14]
    scale = 1.0 / math.sqrt(HD)
    log2_scale = scale * math.log2(math.e)
    rows = queries[0].shape[1]
    slab = 4 * rows
    heads = [slice(h * HD, (h + 1) * HD) for h in range(ABREAST)]

    def window(which, head):
        return jnp.concatenate([ref[:, which, :, head].reshape(slab, HD) for ref in windows], axis=0)

    def tokens(which, head):
        return jnp.concatenate([m[which, :, head] for m in queries], axis=0)

    def each(function, *lists):
        return [function(*one) for one in zip(*lists)]

    nt = (((1,), (1,)), ((), ()))
    nn = (((1,), (0,)), ((), ()))
    tn = (((0,), (0,)), ((), ()))
    dot = functools.partial(lax.dot_general, preferred_element_type=jnp.float32)
    keys, vals = [window(0, h) for h in heads], [window(1, h) for h in heads]
    query, grad = [tokens(0, h) for h in heads], [tokens(1, h) for h in heads]
    scores = each(lambda q, k: dot(q, k, nt) + bias_ref[...], query, keys)
    dweights = each(lambda g, v: dot(g, v, nt), grad, vals)
    peak = each(lambda s: jnp.max(s, axis=1, keepdims=True), scores)
    weights = each(lambda s, m: jnp.exp2((s - m) * log2_scale), scores, peak)
    weights = each(lambda w: w * (1.0 / jnp.sum(w, axis=1, keepdims=True)), weights)
    weights_low = each(lambda w: w.astype(BF16), weights)
    out = each(lambda w, v: dot(w, v, nn).astype(BF16), weights_low, vals)
    out_dot = each(
        lambda g, o: jnp.sum(g.astype(jnp.float32) * o.astype(jnp.float32), axis=1, keepdims=True), grad, out
    )
    dscores = each(lambda w, d, o: (w * (d - o)).astype(BF16), weights, dweights, out_dot)
    for h, head in enumerate(heads):
        dquery = (dot(dscores[h], keys[h], nn) * scale).astype(BF16)
        for i, ref in enumerate(oq_refs):
            ref[0, :, head] = out[h][i * rows : (i + 1) * rows]
            ref[1, :, head] = dquery[i * rows : (i + 1) * rows]
        grads = (dot(dscores[h], query[h], tn) * scale, dot(weights_low[h], grad[h], tn))
        for which, value in enumerate(grads):
            for third, ref in enumerate(grad_refs):
                piece = value[third * slab : (third + 1) * slab]
                ref[:, which, :, head] = piece.reshape(4, rows, HD).astype(BF16)


def attend(bias, queries, own, other, halo):
    _, _, rows, width = own.shape
    heads = width // HD
    block = ABREAST * HD
    two = pl.BlockSpec((2, rows, block), lambda h: (0, 0, h))
    joined = pl.BlockSpec((4, 2, rows, block), lambda h: (0, 0, 0, h))
    pairs = bias.shape[0] * bias.shape[1] * heads
    shapes = [jax.ShapeDtypeStruct((2, rows, width), BF16)] * 4
    shapes += [jax.ShapeDtypeStruct((4, 2, rows, width), BF16)] * 3
    outs = pl.pallas_call(
        attend_kernel,
        grid=(heads // ABREAST,),
        in_specs=[pl.BlockSpec(bias.shape, lambda h: (0, 0))] + [two] * 4 + [joined] * 3,
        out_specs=[two] * 4 + [joined] * 3,
        out_shape=shapes,
        compiler_params=limit(40),
        cost_estimate=pl.CostEstimate(flops=12 * pairs * HD, bytes_accessed=16 * MIB, transcendentals=pairs),
    )(bias, *queries, own, other, halo)
    return list(outs[:4]), outs[4], outs[5], outs[6]


def total_kernel(own_ref, other_ref, halo_ref, *outs):
    for i, ref in enumerate(outs):
        total = own_ref[i].astype(jnp.float32) + other_ref[i].astype(jnp.float32) + halo_ref[i].astype(jnp.float32)
        ref[...] = total.astype(BF16)


def total(own, other, halo):
    _, _, rows, width = own.shape
    piece = HD * 2
    joined = pl.BlockSpec((4, 2, rows, piece), lambda k: (0, 0, 0, k))
    return pl.pallas_call(
        total_kernel,
        grid=(width // piece,),
        in_specs=[joined] * 3,
        out_specs=[pl.BlockSpec((2, rows, piece), lambda k: (0, 0, k))] * 4,
        out_shape=[jax.ShapeDtypeStruct((2, rows, width), BF16)] * 4,
        compiler_params=limit(8),
        cost_estimate=pl.CostEstimate(flops=own.size * 2, bytes_accessed=own.size * 10, transcendentals=0),
    )(own, other, halo)


def bias_kernel(rows, ids_ref, bias_ref):
    tiles, entries = ids_ref.shape
    rings = lax.axis_size("row")
    core, pair, row = lax.axis_index("core"), lax.axis_index("pair"), lax.axis_index("row")
    first = (lax.axis_index("group") * 2 + core - 1) * tiles
    near = jnp.where(core == 0, 2 * tiles, 0)
    blocks = [lax.rem(row - b + rings, rings) * 2 + (pair ^ a) for a, b in SHIFTS]
    token = lax.broadcasted_iota(jnp.int32, (1, rows), 1)
    own = jnp.concatenate([(token + block * rows) // TILE for block in blocks], axis=1)
    columns = jnp.concatenate([own + tiles, own + near, own + 2 * tiles - near], axis=1) + first
    lists = []
    for t in range(tiles):
        listed = columns < 0
        for n in range(entries):
            key = ids_ref[t, n]
            listed = listed | (columns == jnp.where(key >= 0, key, -7 * tiles))
        lists.append(jnp.where(listed & (columns >= 0), 0.0, MASKED))
    token = lax.broadcasted_iota(jnp.int32, (rows, 1), 0)
    for i, block in enumerate(blocks):
        tile = (token + block * rows) // TILE
        bias = jnp.broadcast_to(lists[0], (rows, columns.shape[1]))
        for t in range(1, tiles):
            bias = jnp.where(tile == t, lists[t], bias)
        bias_ref[i * rows : (i + 1) * rows] = bias


def slab_ids(neighbours):
    rings = lax.axis_size("row")
    swap = []
    for p in range(2):
        for r in range(rings):
            for c in range(2):
                swap.append(((p * rings + r) * 2 + c, (c * rings + r) * 2 + p))
    return lax.ppermute(neighbours, PLANE, swap)


def window_bias(ids, rows):
    slab = 4 * rows
    return pl.pallas_call(
        functools.partial(bias_kernel, rows),
        in_specs=[pl.BlockSpec(memory_space=pltpu.SMEM)],
        out_specs=pl.BlockSpec(memory_space=pltpu.VMEM),
        out_shape=jax.ShapeDtypeStruct((slab, 3 * slab), jnp.float32),
        compiler_params=limit(8),
        cost_estimate=pl.CostEstimate(flops=20 * slab * slab, bytes_accessed=12 * slab * slab, transcendentals=0),
    )(ids)


def per_device(query_in, key_in, value_in, grad_out, neighbours):
    groups, rings = lax.axis_size("group"), lax.axis_size("row")
    rows, full_width = query_in.shape
    group_width = full_width // (2 * rings)

    def place(g, p, r, c):
        return ((g * 2 + p) * rings + r) * 2 + c

    everyone = [(g, p, r, c) for g in range(groups) for p in range(2) for r in range(rings) for c in range(2)]

    def spread_pairs(shift):
        a, b = shift
        return [(place(g, p, r, c), place(g, c ^ a, (r + b) % rings, p)) for g, p, r, c in everyone]

    beside = []
    for g, p, r, c in everyone:
        to = g + 1 if c == 1 else g - 1
        inside = 0 <= to < groups
        beside.append((place(g, p, r, c), place(to, p, r, 1 - c) if inside else place(g, p, r, c)))

    def send(messages):
        return [lax.ppermute(m, AXES, spread_pairs(s)) for m, s in zip(messages, SHIFTS)]

    def send_back(messages):
        return [
            lax.ppermute(m, AXES, [(d, s) for s, d in spread_pairs(shift)]) for m, shift in zip(messages, SHIFTS)
        ]

    def across(x):
        return lax.ppermute(x, "core", [(0, 1), (1, 0)])

    def halo(x):
        return lax.ppermute(x, AXES, beside)

    key_out = pack(key_in, value_in, group_width)
    key_out, query_in, neighbours = lax.optimization_barrier((key_out, query_in, neighbours))
    query_out = list(pack(query_in, grad_out, group_width))
    owns, ids = lax.optimization_barrier((send(key_out), slab_ids(neighbours)))
    own = join(owns)
    query_out[EARLY:], own = lax.optimization_barrier((query_out[EARLY:], own))
    other = across(own)
    query_out[3], other = lax.optimization_barrier((query_out[3], other))
    far = halo(own)
    queries = send(query_out)
    bias = window_bias(ids, rows)
    oq, own_part, other_part, far_part = attend(bias, queries, own, other, far)
    other_part = across(other_part)
    other_part, oq[3] = lax.optimization_barrier((other_part, oq[3]))
    grads = total(own_part, other_part, halo(far_part))
    forward = unpack(send_back(oq), full_width)
    return *forward, *unpack(send_back(grads), full_width)


def solution(mesh):
    slabs, heads = mesh.devices.shape
    paired = Mesh(mesh.devices.reshape(slabs // 2, 2, heads // 2, 2), AXES)
    tokens = P(AXES, None)
    return jax.shard_map(
        per_device,
        mesh=paired,
        in_specs=(tokens, tokens, tokens, tokens, P(("group", "pair"), None)),
        out_specs=(tokens, tokens, tokens, tokens),
        check_vma=False,
    )
```

```python
import functools
import math

import jax
import jax.numpy as jnp
from jax import lax
from jax.experimental import pallas as pl
from jax.experimental.pallas import tpu as pltpu
from jax.sharding import Mesh
from jax.sharding import PartitionSpec as P

HD = 128
TILE = 64
EARLY = 1
ABREAST = 2
MASKED = -1e30
AXES = ("group", "pair", "row", "core")
PLANE = ("pair", "row", "core")
SHIFTS = ((1, 1), (0, 0), (0, 1), (1, 0))
BF16 = jnp.bfloat16
ANY = pl.BlockSpec(memory_space=pl.ANY)
FAR = pl.BlockSpec(memory_space=pltpu.HBM)
NEAR = pl.BlockSpec(memory_space=pltpu.VMEM)


def run_copies(copies):
    for copy in copies:
        copy.start()
    for copy in copies:
        copy.wait()


def head_group(shift):
    a, b = shift
    rows = lax.axis_size("row")
    return (lax.axis_index("core") ^ a) * rows + lax.rem(lax.axis_index("row") + b, rows)


MIB = 1024 * 1024


def limit(mib):
    return pltpu.CompilerParams(vmem_limit_bytes=mib * MIB)


def pack_kernel(first, second, *refs):
    messages, sem = refs[:4], refs[4]
    width = messages[0].shape[2]
    copies = []
    for i, message in enumerate(messages):
        columns = pl.ds(pl.multiple_of(head_group(SHIFTS[i]) * width, HD), width)
        for j, array in enumerate((first, second)):
            copies.append(pltpu.make_async_copy(array.at[:, columns], message.at[j], sem.at[i, j]))
    run_copies(copies)


def pack(first, second, group_width):
    rows = first.shape[0]
    return pl.pallas_call(
        pack_kernel,
        in_specs=[FAR, FAR],
        out_specs=[NEAR] * 4,
        out_shape=[jax.ShapeDtypeStruct((2, rows, group_width), BF16)] * 4,
        scratch_shapes=[pltpu.SemaphoreType.DMA((4, 2))],
        compiler_params=limit(8),
        cost_estimate=pl.CostEstimate(flops=0, bytes_accessed=32 * rows * group_width, transcendentals=0),
    )(first, second)


def unpack_kernel(*refs):
    messages, arrays, sem = refs[:4], refs[4:6], refs[6]
    width = messages[0].shape[2]
    copies = []
    for i, message in enumerate(messages):
        columns = pl.ds(pl.multiple_of(head_group(SHIFTS[i]) * width, HD), width)
        for j, array in enumerate(arrays):
            copies.append(pltpu.make_async_copy(message.at[j], array.at[:, columns], sem.at[i, j]))
    run_copies(copies)


def unpack(messages, full_width):
    _, rows, width = messages[0].shape
    return pl.pallas_call(
        unpack_kernel,
        in_specs=[NEAR] * 4,
        out_specs=[ANY] * 2,
        out_shape=[jax.ShapeDtypeStruct((rows, full_width), BF16)] * 2,
        scratch_shapes=[pltpu.SemaphoreType.DMA((4, 2))],
        compiler_params=limit(8),
        cost_estimate=pl.CostEstimate(flops=0, bytes_accessed=8 * rows * full_width, transcendentals=0),
    )(*messages)


def join_kernel(*refs):
    run_copies([pltpu.make_async_copy(m, refs[4].at[i], refs[5].at[i]) for i, m in enumerate(refs[:4])])


def join(messages):
    _, rows, width = messages[0].shape
    return pl.pallas_call(
        join_kernel,
        in_specs=[NEAR] * 4,
        out_specs=NEAR,
        out_shape=jax.ShapeDtypeStruct((4, 2, rows, width), BF16),
        scratch_shapes=[pltpu.SemaphoreType.DMA((4,))],
        compiler_params=limit(8),
        cost_estimate=pl.CostEstimate(flops=0, bytes_accessed=32 * rows * width, transcendentals=0),
    )(*messages)


def attend_kernel(bias_ref, *refs):
    queries, windows = refs[:4], refs[4:7]
    oq_refs, grad_refs = refs[7:11], refs[11:14]
    scale = 1.0 / math.sqrt(HD)
    log2_scale = scale * math.log2(math.e)
    rows = queries[0].shape[1]
    slab = 4 * rows
    count = queries[0].shape[2] // HD
    for first in range(0, count, ABREAST):
        heads = [slice(h * HD, (h + 1) * HD) for h in range(first, first + ABREAST)]
        attend_heads(heads, bias_ref, queries, windows, oq_refs, grad_refs, rows, slab, scale, log2_scale)


def attend_heads(heads, bias_ref, queries, windows, oq_refs, grad_refs, rows, slab, scale, log2_scale):

    def window(which, head):
        return jnp.concatenate([ref[:, which, :, head].reshape(slab, HD) for ref in windows], axis=0)

    def tokens(which, head):
        return jnp.concatenate([m[which, :, head] for m in queries], axis=0)

    def each(function, *lists):
        return [function(*one) for one in zip(*lists)]

    nt = (((1,), (1,)), ((), ()))
    nn = (((1,), (0,)), ((), ()))
    tn = (((0,), (0,)), ((), ()))
    dot = functools.partial(lax.dot_general, preferred_element_type=jnp.float32)
    keys, vals = [window(0, h) for h in heads], [window(1, h) for h in heads]
    query, grad = [tokens(0, h) for h in heads], [tokens(1, h) for h in heads]
    scores = each(lambda q, k: dot(q, k, nt) + bias_ref[...], query, keys)
    dweights = each(lambda g, v: dot(g, v, nt), grad, vals)
    peak = each(lambda s: jnp.max(s, axis=1, keepdims=True), scores)
    weights = each(lambda s, m: jnp.exp2((s - m) * log2_scale), scores, peak)
    weights = each(lambda w: w * (1.0 / jnp.sum(w, axis=1, keepdims=True)), weights)
    weights_low = each(lambda w: w.astype(BF16), weights)
    out = each(lambda w, v: dot(w, v, nn).astype(BF16), weights_low, vals)
    out_dot = each(
        lambda g, o: jnp.sum(g.astype(jnp.float32) * o.astype(jnp.float32), axis=1, keepdims=True), grad, out
    )
    dscores = each(lambda w, d, o: (w * (d - o)).astype(BF16), weights, dweights, out_dot)
    for h, head in enumerate(heads):
        dquery = (dot(dscores[h], keys[h], nn) * scale).astype(BF16)
        for i, ref in enumerate(oq_refs):
            ref[0, :, head] = out[h][i * rows : (i + 1) * rows]
            ref[1, :, head] = dquery[i * rows : (i + 1) * rows]
        grads = (dot(dscores[h], query[h], tn) * scale, dot(weights_low[h], grad[h], tn))
        for which, value in enumerate(grads):
            for third, ref in enumerate(grad_refs):
                piece = value[third * slab : (third + 1) * slab]
                ref[:, which, :, head] = piece.reshape(4, rows, HD).astype(BF16)


def attend(bias, queries, own, other, halo):
    _, _, rows, width = own.shape
    heads = width // HD
    pairs = bias.shape[0] * bias.shape[1] * heads
    shapes = [jax.ShapeDtypeStruct((2, rows, width), BF16)] * 4
    shapes += [jax.ShapeDtypeStruct((4, 2, rows, width), BF16)] * 3
    outs = pl.pallas_call(
        attend_kernel,
        in_specs=[NEAR] * 8,
        out_specs=[NEAR] * 7,
        out_shape=shapes,
        compiler_params=limit(32),
        cost_estimate=pl.CostEstimate(flops=12 * pairs * HD, bytes_accessed=16 * MIB, transcendentals=pairs),
    )(bias, *queries, own, other, halo)
    return list(outs[:4]), outs[4], outs[5], outs[6]


def total_kernel(own_ref, other_ref, halo_ref, *outs):
    for i, ref in enumerate(outs):
        total = own_ref[i].astype(jnp.float32) + other_ref[i].astype(jnp.float32) + halo_ref[i].astype(jnp.float32)
        ref[...] = total.astype(BF16)


def total(own, other, halo):
    _, _, rows, width = own.shape
    return pl.pallas_call(
        total_kernel,
        in_specs=[NEAR] * 3,
        out_specs=[NEAR] * 4,
        out_shape=[jax.ShapeDtypeStruct((2, rows, width), BF16)] * 4,
        compiler_params=limit(12),
        cost_estimate=pl.CostEstimate(flops=own.size * 2, bytes_accessed=own.size * 8, transcendentals=0),
    )(own, other, halo)


def bias_kernel(rows, ids_ref, bias_ref):
    tiles, entries = ids_ref.shape
    rings = lax.axis_size("row")
    core, pair, row = lax.axis_index("core"), lax.axis_index("pair"), lax.axis_index("row")
    first = (lax.axis_index("group") * 2 + core - 1) * tiles
    near = jnp.where(core == 0, 2 * tiles, 0)
    blocks = [lax.rem(row - b + rings, rings) * 2 + (pair ^ a) for a, b in SHIFTS]
    token = lax.broadcasted_iota(jnp.int32, (1, rows), 1)
    own = jnp.concatenate([(token + block * rows) // TILE for block in blocks], axis=1)
    columns = jnp.concatenate([own + tiles, own + near, own + 2 * tiles - near], axis=1) + first
    lists = []
    for t in range(tiles):
        listed = columns < 0
        for n in range(entries):
            key = ids_ref[t, n]
            listed = listed | (columns == jnp.where(key >= 0, key, -7 * tiles))
        lists.append(jnp.where(listed & (columns >= 0), 0.0, MASKED))
    token = lax.broadcasted_iota(jnp.int32, (rows, 1), 0)
    for i, block in enumerate(blocks):
        tile = (token + block * rows) // TILE
        bias = jnp.broadcast_to(lists[0], (rows, columns.shape[1]))
        for t in range(1, tiles):
            bias = jnp.where(tile == t, lists[t], bias)
        bias_ref[i * rows : (i + 1) * rows] = bias


def slab_ids(neighbours):
    rings = lax.axis_size("row")
    swap = []
    for p in range(2):
        for r in range(rings):
            for c in range(2):
                swap.append(((p * rings + r) * 2 + c, (c * rings + r) * 2 + p))
    return lax.ppermute(neighbours, PLANE, swap)


def window_bias(ids, rows):
    slab = 4 * rows
    return pl.pallas_call(
        functools.partial(bias_kernel, rows),
        in_specs=[pl.BlockSpec(memory_space=pltpu.SMEM)],
        out_specs=pl.BlockSpec(memory_space=pltpu.VMEM),
        out_shape=jax.ShapeDtypeStruct((slab, 3 * slab), jnp.float32),
        compiler_params=limit(8),
        cost_estimate=pl.CostEstimate(flops=20 * slab * slab, bytes_accessed=12 * slab * slab, transcendentals=0),
    )(ids)


def per_device(query_in, key_in, value_in, grad_out, neighbours):
    groups, rings = lax.axis_size("group"), lax.axis_size("row")
    rows, full_width = query_in.shape
    group_width = full_width // (2 * rings)

    def place(g, p, r, c):
        return ((g * 2 + p) * rings + r) * 2 + c

    everyone = [(g, p, r, c) for g in range(groups) for p in range(2) for r in range(rings) for c in range(2)]

    def spread_pairs(shift):
        a, b = shift
        return [(place(g, p, r, c), place(g, c ^ a, (r + b) % rings, p)) for g, p, r, c in everyone]

    beside = []
    for g, p, r, c in everyone:
        to = g + 1 if c == 1 else g - 1
        inside = 0 <= to < groups
        beside.append((place(g, p, r, c), place(to, p, r, 1 - c) if inside else place(g, p, r, c)))

    def send(messages):
        return [lax.ppermute(m, AXES, spread_pairs(s)) for m, s in zip(messages, SHIFTS)]

    def send_back(messages):
        return [
            lax.ppermute(m, AXES, [(d, s) for s, d in spread_pairs(shift)]) for m, shift in zip(messages, SHIFTS)
        ]

    def across(x):
        return lax.ppermute(x, "core", [(0, 1), (1, 0)])

    def halo(x):
        return lax.ppermute(x, AXES, beside)

    key_out = pack(key_in, value_in, group_width)
    key_out, query_in, neighbours = lax.optimization_barrier((key_out, query_in, neighbours))
    query_out = list(pack(query_in, grad_out, group_width))
    owns, ids = lax.optimization_barrier((send(key_out), slab_ids(neighbours)))
    own = join(owns)
    query_out[EARLY:], own = lax.optimization_barrier((query_out[EARLY:], own))
    other = across(own)
    query_out[3], other = lax.optimization_barrier((query_out[3], other))
    far = halo(own)
    queries = send(query_out)
    bias = window_bias(ids, rows)
    oq, own_part, other_part, far_part = attend(bias, queries, own, other, far)
    other_part = across(other_part)
    other_part, oq[3] = lax.optimization_barrier((other_part, oq[3]))
    grads = total(own_part, other_part, halo(far_part))
    forward = unpack(send_back(oq), full_width)
    return *forward, *unpack(send_back(grads), full_width)


def solution(mesh):
    slabs, heads = mesh.devices.shape
    paired = Mesh(mesh.devices.reshape(slabs // 2, 2, heads // 2, 2), AXES)
    tokens = P(AXES, None)
    return jax.shard_map(
        per_device,
        mesh=paired,
        in_specs=(tokens, tokens, tokens, tokens, P(("group", "pair"), None)),
        out_specs=(tokens, tokens, tokens, tokens),
        check_vma=False,
    )
```

```python
import functools
import math

import jax
import jax.numpy as jnp
from jax import lax
from jax.experimental import pallas as pl
from jax.experimental.pallas import tpu as pltpu
from jax.sharding import Mesh
from jax.sharding import PartitionSpec as P

HD = 128
TILE = 64
BACK = (3, 2, 0, 1)
EARLY = 1
MASKED = -1e30
AXES = ("group", "pair", "row", "core")
PLANE = ("pair", "row", "core")
SHIFTS = ((1, 1), (0, 0), (0, 1), (1, 0))
BF16 = jnp.bfloat16
ANY = pl.BlockSpec(memory_space=pl.ANY)
FAR = pl.BlockSpec(memory_space=pltpu.HBM)
NEAR = pl.BlockSpec(memory_space=pltpu.VMEM)


def run_copies(copies):
    for copy in copies:
        copy.start()
    for copy in copies:
        copy.wait()


def head_group(shift):
    a, b = shift
    rows = lax.axis_size("row")
    return (lax.axis_index("core") ^ a) * rows + lax.rem(lax.axis_index("row") + b, rows)


MIB = 1024 * 1024


def limit(mib):
    return pltpu.CompilerParams(vmem_limit_bytes=mib * MIB)


def pack_kernel(first, second, *refs):
    messages, sem = refs[:4], refs[4]
    width = messages[0].shape[2]
    copies = []
    for i, message in enumerate(messages):
        columns = pl.ds(pl.multiple_of(head_group(SHIFTS[i]) * width, HD), width)
        for j, array in enumerate((first, second)):
            copies.append(pltpu.make_async_copy(array.at[:, columns], message.at[j], sem.at[i, j]))
    run_copies(copies)


def pack(first, second, group_width):
    rows = first.shape[0]
    return pl.pallas_call(
        pack_kernel,
        in_specs=[FAR, FAR],
        out_specs=[NEAR] * 4,
        out_shape=[jax.ShapeDtypeStruct((2, rows, group_width), BF16)] * 4,
        scratch_shapes=[pltpu.SemaphoreType.DMA((4, 2))],
        compiler_params=limit(8),
        cost_estimate=pl.CostEstimate(flops=0, bytes_accessed=32 * rows * group_width, transcendentals=0),
    )(first, second)


def unpack_kernel(order, *refs):
    messages, arrays, sem = refs[:4], refs[4:6], refs[6]
    width = messages[0].shape[2]
    copies = []
    for i, message in enumerate(messages):
        columns = pl.ds(pl.multiple_of(head_group(SHIFTS[order[i]]) * width, HD), width)
        for j, array in enumerate(arrays):
            copies.append(pltpu.make_async_copy(message.at[j], array.at[:, columns], sem.at[i, j]))
    run_copies(copies)


def unpack(messages, full_width, order=(0, 1, 2, 3)):
    _, rows, width = messages[0].shape
    return pl.pallas_call(
        functools.partial(unpack_kernel, order),
        in_specs=[NEAR] * 4,
        out_specs=[ANY] * 2,
        out_shape=[jax.ShapeDtypeStruct((rows, full_width), BF16)] * 2,
        scratch_shapes=[pltpu.SemaphoreType.DMA((4, 2))],
        compiler_params=limit(8),
        cost_estimate=pl.CostEstimate(flops=0, bytes_accessed=8 * rows * full_width, transcendentals=0),
    )(*(messages[i] for i in order))


def join_kernel(*refs):
    run_copies([pltpu.make_async_copy(m, refs[4].at[i], refs[5].at[i]) for i, m in enumerate(refs[:4])])


def join(messages):
    _, rows, width = messages[0].shape
    return pl.pallas_call(
        join_kernel,
        in_specs=[NEAR] * 4,
        out_specs=NEAR,
        out_shape=jax.ShapeDtypeStruct((4, 2, rows, width), BF16),
        scratch_shapes=[pltpu.SemaphoreType.DMA((4,))],
        compiler_params=limit(8),
        cost_estimate=pl.CostEstimate(flops=0, bytes_accessed=32 * rows * width, transcendentals=0),
    )(*messages)


def attend_kernel(bias_ref, *refs):
    queries, windows = refs[:4], refs[4:7]
    oq_refs, grad_refs = refs[7:11], refs[11:14]
    scale = 1.0 / math.sqrt(HD)
    log2_scale = scale * math.log2(math.e)
    rows, width = queries[0].shape[1:]
    slab = 4 * rows
    nt = (((1,), (1,)), ((), ()))
    nn = (((1,), (0,)), ((), ()))
    tn = (((0,), (0,)), ((), ()))
    dot = functools.partial(lax.dot_general, preferred_element_type=jnp.float32)

    def window(which, head):
        return jnp.concatenate([ref[:, which, :, head].reshape(slab, HD) for ref in windows], axis=0)

    def tokens(which, head):
        return jnp.concatenate([m[which, :, head] for m in queries], axis=0)

    def products(head):
        scores = dot(tokens(0, head), window(0, head), nt) + bias_ref[...]
        return scores, dot(tokens(1, head), window(1, head), nt)

    def softmax(scores):
        peak = jnp.max(scores, axis=1, keepdims=True)
        weights = jnp.exp2((scores - peak) * log2_scale)
        return weights * (1.0 / jnp.sum(weights, axis=1, keepdims=True))

    def attended(head, weights_low):
        out = dot(weights_low, window(1, head), nn).astype(BF16)
        for i, ref in enumerate(oq_refs):
            ref[0, :, head] = out[i * rows : (i + 1) * rows]
        grad = tokens(1, head).astype(jnp.float32)
        return jnp.sum(grad * out.astype(jnp.float32), axis=1, keepdims=True)

    def store(which, head, value):
        for third, ref in enumerate(grad_refs):
            piece = value[third * slab : (third + 1) * slab]
            ref[:, which, :, head] = piece.reshape(4, rows, HD).astype(BF16)

    def value_grad(head, weights_low):
        store(1, head, dot(weights_low, tokens(1, head), tn))

    def other_grads(head, dscores):
        dquery = (dot(dscores, window(0, head), nn) * scale).astype(BF16)
        for i, ref in enumerate(oq_refs):
            ref[1, :, head] = dquery[i * rows : (i + 1) * rows]
        store(0, head, dot(dscores, tokens(0, head), tn) * scale)

    heads = [slice(h, h + HD) for h in range(0, width, HD)]
    for i in range(0, len(heads), 2):
        pair = heads[i : i + 2]
        ready = [products(h) for h in pair]
        weights = [softmax(s) for s, _ in ready]
        low = [w.astype(BF16) for w in weights]
        out_dot = [attended(h, l) for h, l in zip(pair, low)]
        for h, l in zip(pair, low):
            value_grad(h, l)
        dscores = [(w * (r[1] - o)).astype(BF16) for w, r, o in zip(weights, ready, out_dot)]
        for h, d in zip(pair, dscores):
            other_grads(h, d)

def attend(bias, queries, own, other, halo):
    _, _, rows, width = own.shape
    heads = width // HD
    pairs = bias.shape[0] * bias.shape[1] * heads
    shapes = [jax.ShapeDtypeStruct((2, rows, width), BF16)] * 4
    shapes += [jax.ShapeDtypeStruct((4, 2, rows, width), BF16)] * 3
    outs = pl.pallas_call(
        attend_kernel,
        in_specs=[NEAR] * 8,
        out_specs=[NEAR] * 7,
        out_shape=shapes,
        compiler_params=limit(32),
        cost_estimate=pl.CostEstimate(flops=12 * pairs * HD, bytes_accessed=16 * MIB, transcendentals=pairs),
    )(bias, *queries, own, other, halo)
    return list(outs[:4]), outs[4], outs[5], outs[6]


def total_kernel(own_ref, other_ref, halo_ref, *outs):
    for i, ref in enumerate(outs):
        total = own_ref[i].astype(jnp.float32) + other_ref[i].astype(jnp.float32) + halo_ref[i].astype(jnp.float32)
        ref[...] = total.astype(BF16)


def total(own, other, halo):
    _, _, rows, width = own.shape
    return pl.pallas_call(
        total_kernel,
        in_specs=[NEAR] * 3,
        out_specs=[NEAR] * 4,
        out_shape=[jax.ShapeDtypeStruct((2, rows, width), BF16)] * 4,
        compiler_params=limit(12),
        cost_estimate=pl.CostEstimate(flops=own.size * 2, bytes_accessed=own.size * 8, transcendentals=0),
    )(own, other, halo)


def bias_kernel(rows, ids_ref, bias_ref):
    tiles, entries = ids_ref.shape
    rings = lax.axis_size("row")
    core, pair, row = lax.axis_index("core"), lax.axis_index("pair"), lax.axis_index("row")
    first = (lax.axis_index("group") * 2 + core - 1) * tiles
    near = jnp.where(core == 0, 2 * tiles, 0)
    blocks = [lax.rem(row - b + rings, rings) * 2 + (pair ^ a) for a, b in SHIFTS]
    token = lax.broadcasted_iota(jnp.int32, (1, rows), 1)
    own = jnp.concatenate([(token + block * rows) // TILE for block in blocks], axis=1)
    columns = jnp.concatenate([own + tiles, own + near, own + 2 * tiles - near], axis=1) + first
    lists = []
    for t in range(tiles):
        listed = columns < 0
        for n in range(entries):
            key = ids_ref[t, n]
            listed = listed | (columns == jnp.where(key >= 0, key, -7 * tiles))
        lists.append(jnp.where(listed & (columns >= 0), 0.0, MASKED))
    token = lax.broadcasted_iota(jnp.int32, (rows, 1), 0)
    for i, block in enumerate(blocks):
        tile = (token + block * rows) // TILE
        bias = jnp.broadcast_to(lists[0], (rows, columns.shape[1]))
        for t in range(1, tiles):
            bias = jnp.where(tile == t, lists[t], bias)
        bias_ref[i * rows : (i + 1) * rows] = bias


def slab_ids(neighbours):
    rings = lax.axis_size("row")
    swap = []
    for p in range(2):
        for r in range(rings):
            for c in range(2):
                swap.append(((p * rings + r) * 2 + c, (c * rings + r) * 2 + p))
    return lax.ppermute(neighbours, PLANE, swap)


def window_bias(ids, rows):
    slab = 4 * rows
    return pl.pallas_call(
        functools.partial(bias_kernel, rows),
        in_specs=[pl.BlockSpec(memory_space=pltpu.SMEM)],
        out_specs=pl.BlockSpec(memory_space=pltpu.VMEM),
        out_shape=jax.ShapeDtypeStruct((slab, 3 * slab), jnp.float32),
        compiler_params=limit(8),
        cost_estimate=pl.CostEstimate(flops=20 * slab * slab, bytes_accessed=12 * slab * slab, transcendentals=0),
    )(ids)


def per_device(query_in, key_in, value_in, grad_out, neighbours):
    groups, rings = lax.axis_size("group"), lax.axis_size("row")
    rows, full_width = query_in.shape
    group_width = full_width // (2 * rings)

    def place(g, p, r, c):
        return ((g * 2 + p) * rings + r) * 2 + c

    everyone = [(g, p, r, c) for g in range(groups) for p in range(2) for r in range(rings) for c in range(2)]

    def spread_pairs(shift):
        a, b = shift
        return [(place(g, p, r, c), place(g, c ^ a, (r + b) % rings, p)) for g, p, r, c in everyone]

    beside = []
    for g, p, r, c in everyone:
        to = g + 1 if c == 1 else g - 1
        inside = 0 <= to < groups
        beside.append((place(g, p, r, c), place(to, p, r, 1 - c) if inside else place(g, p, r, c)))

    def send(messages):
        return [lax.ppermute(m, AXES, spread_pairs(s)) for m, s in zip(messages, SHIFTS)]

    def send_back(messages, order=(0, 1, 2, 3)):
        back = dict.fromkeys(range(4))
        for i in order:
            back[i] = lax.ppermute(messages[i], AXES, [(d, s) for s, d in spread_pairs(SHIFTS[i])])
        return list(back.values())

    def across(x):
        return lax.ppermute(x, "core", [(0, 1), (1, 0)])

    def halo(x):
        return lax.ppermute(x, AXES, beside)

    key_out = pack(key_in, value_in, group_width)
    key_out, query_in, neighbours = lax.optimization_barrier((key_out, query_in, neighbours))
    query_out = list(pack(query_in, grad_out, group_width))
    owns, ids = lax.optimization_barrier((send(key_out), slab_ids(neighbours)))
    own = join(owns)
    query_out[EARLY:], own = lax.optimization_barrier((query_out[EARLY:], own))
    other = across(own)
    query_out[3], other = lax.optimization_barrier((query_out[3], other))
    far = halo(own)
    queries = send(query_out)
    bias = window_bias(ids, rows)
    oq, own_part, other_part, far_part = attend(bias, queries, own, other, far)
    other_part = across(other_part)
    other_part, oq[3] = lax.optimization_barrier((other_part, oq[3]))
    grads = total(own_part, other_part, halo(far_part))
    forward = unpack(send_back(oq, BACK), full_width, BACK)
    return *forward, *unpack(send_back(grads, BACK), full_width, BACK)


def solution(mesh):
    slabs, heads = mesh.devices.shape
    paired = Mesh(mesh.devices.reshape(slabs // 2, 2, heads // 2, 2), AXES)
    tokens = P(AXES, None)
    return jax.shard_map(
        per_device,
        mesh=paired,
        in_specs=(tokens, tokens, tokens, tokens, P(("group", "pair"), None)),
        out_specs=(tokens, tokens, tokens, tokens),
        check_vma=False,
    )
```

```python
import functools
import math

import jax
import jax.numpy as jnp
from jax import lax
from jax.experimental import pallas as pl
from jax.experimental.pallas import tpu as pltpu
from jax.sharding import Mesh
from jax.sharding import PartitionSpec as P

HD = 128
TILE = 64
BACK = (2, 1, 0, 3)
EARLY = 1
MASKED = -1e30
AXES = ("group", "pair", "row", "core")
PLANE = ("pair", "row", "core")
SHIFTS = ((1, 1), (0, 1), (1, 0), (0, 0))
BF16 = jnp.bfloat16
ANY = pl.BlockSpec(memory_space=pl.ANY)
FAR = pl.BlockSpec(memory_space=pltpu.HBM)
NEAR = pl.BlockSpec(memory_space=pltpu.VMEM)


def run_copies(copies):
    for copy in copies:
        copy.start()
    for copy in copies:
        copy.wait()


def head_group(shift):
    a, b = shift
    rows = lax.axis_size("row")
    return (lax.axis_index("core") ^ a) * rows + lax.rem(lax.axis_index("row") + b, rows)


MIB = 1024 * 1024


def limit(mib):
    return pltpu.CompilerParams(vmem_limit_bytes=mib * MIB)


def pack_kernel(first, second, *refs):
    messages, sem = refs[:4], refs[4]
    width = messages[0].shape[2]
    copies = []
    for i, message in enumerate(messages):
        columns = pl.ds(pl.multiple_of(head_group(SHIFTS[i]) * width, HD), width)
        for j, array in enumerate((first, second)):
            copies.append(pltpu.make_async_copy(array.at[:, columns], message.at[j], sem.at[i, j]))
    run_copies(copies)


def pack(first, second, group_width):
    rows = first.shape[0]
    return pl.pallas_call(
        pack_kernel,
        in_specs=[FAR, FAR],
        out_specs=[NEAR] * 4,
        out_shape=[jax.ShapeDtypeStruct((2, rows, group_width), BF16)] * 4,
        scratch_shapes=[pltpu.SemaphoreType.DMA((4, 2))],
        compiler_params=limit(8),
        cost_estimate=pl.CostEstimate(flops=0, bytes_accessed=32 * rows * group_width, transcendentals=0),
    )(first, second)


def unpack_kernel(order, *refs):
    messages, arrays, sem = refs[:4], refs[4:6], refs[6]
    width = messages[0].shape[2]
    copies = []
    for i, message in enumerate(messages):
        columns = pl.ds(pl.multiple_of(head_group(SHIFTS[order[i]]) * width, HD), width)
        for j, array in enumerate(arrays):
            copies.append(pltpu.make_async_copy(message.at[j], array.at[:, columns], sem.at[i, j]))
    run_copies(copies)


def unpack(messages, full_width, order=(0, 1, 2, 3)):
    _, rows, width = messages[0].shape
    return pl.pallas_call(
        functools.partial(unpack_kernel, order),
        in_specs=[NEAR] * 4,
        out_specs=[ANY] * 2,
        out_shape=[jax.ShapeDtypeStruct((rows, full_width), BF16)] * 2,
        scratch_shapes=[pltpu.SemaphoreType.DMA((4, 2))],
        compiler_params=limit(8),
        cost_estimate=pl.CostEstimate(flops=0, bytes_accessed=8 * rows * full_width, transcendentals=0),
    )(*(messages[i] for i in order))


def join_kernel(*refs):
    run_copies([pltpu.make_async_copy(m, refs[4].at[i], refs[5].at[i]) for i, m in enumerate(refs[:4])])


def join(messages):
    _, rows, width = messages[0].shape
    return pl.pallas_call(
        join_kernel,
        in_specs=[NEAR] * 4,
        out_specs=NEAR,
        out_shape=jax.ShapeDtypeStruct((4, 2, rows, width), BF16),
        scratch_shapes=[pltpu.SemaphoreType.DMA((4,))],
        compiler_params=limit(8),
        cost_estimate=pl.CostEstimate(flops=0, bytes_accessed=32 * rows * width, transcendentals=0),
    )(*messages)


def attend_kernel(bias_ref, *refs):
    queries, windows = refs[:4], refs[4:7]
    oq_refs, grad_refs = refs[7:11], refs[11:14]
    scale = 1.0 / math.sqrt(HD)
    log2_scale = scale * math.log2(math.e)
    rows, width = queries[0].shape[1:]
    slab = 4 * rows
    nt = (((1,), (1,)), ((), ()))
    nn = (((1,), (0,)), ((), ()))
    tn = (((0,), (0,)), ((), ()))
    dot = functools.partial(lax.dot_general, preferred_element_type=jnp.float32)

    def window(which, head):
        return jnp.concatenate([ref[:, which, :, head].reshape(slab, HD) for ref in windows], axis=0)

    def tokens(which, head):
        return jnp.concatenate([m[which, :, head] for m in queries], axis=0)

    def products(head):
        scores = dot(tokens(0, head), window(0, head), nt) + bias_ref[...]
        return scores, dot(tokens(1, head), window(1, head), nt)

    def softmax(scores):
        peak = jnp.max(scores, axis=1, keepdims=True)
        weights = jnp.exp2((scores - peak) * log2_scale)
        return weights * (1.0 / jnp.sum(weights, axis=1, keepdims=True))

    def attended(head, weights_low):
        out = dot(weights_low, window(1, head), nn).astype(BF16)
        for i, ref in enumerate(oq_refs):
            ref[0, :, head] = out[i * rows : (i + 1) * rows]
        grad = tokens(1, head).astype(jnp.float32)
        return jnp.sum(grad * out.astype(jnp.float32), axis=1, keepdims=True)

    def store(which, head, value):
        for third, ref in enumerate(grad_refs):
            piece = value[third * slab : (third + 1) * slab]
            ref[:, which, :, head] = piece.reshape(4, rows, HD).astype(BF16)

    def value_grad(head, weights_low):
        store(1, head, dot(weights_low, tokens(1, head), tn))

    def other_grads(head, dscores):
        dquery = (dot(dscores, window(0, head), nn) * scale).astype(BF16)
        for i, ref in enumerate(oq_refs):
            ref[1, :, head] = dquery[i * rows : (i + 1) * rows]
        store(0, head, dot(dscores, tokens(0, head), tn) * scale)

    heads = [slice(h, h + HD) for h in range(0, width, HD)]
    for i in range(0, len(heads), 2):
        pair = heads[i : i + 2]
        ready = [products(h) for h in pair]
        weights = [softmax(s) for s, _ in ready]
        low = [w.astype(BF16) for w in weights]
        out_dot = [attended(h, l) for h, l in zip(pair, low)]
        for h, l in zip(pair, low):
            value_grad(h, l)
        dscores = [(w * (r[1] - o)).astype(BF16) for w, r, o in zip(weights, ready, out_dot)]
        for h, d in zip(pair, dscores):
            other_grads(h, d)

def attend(bias, queries, own, other, halo):
    _, _, rows, width = own.shape
    heads = width // HD
    pairs = bias.shape[0] * bias.shape[1] * heads
    shapes = [jax.ShapeDtypeStruct((2, rows, width), BF16)] * 4
    shapes += [jax.ShapeDtypeStruct((4, 2, rows, width), BF16)] * 3
    outs = pl.pallas_call(
        attend_kernel,
        in_specs=[NEAR] * 8,
        out_specs=[NEAR] * 7,
        out_shape=shapes,
        compiler_params=limit(32),
        cost_estimate=pl.CostEstimate(flops=12 * pairs * HD, bytes_accessed=16 * MIB, transcendentals=pairs),
    )(bias, *queries, own, other, halo)
    return list(outs[:4]), outs[4], outs[5], outs[6]


def total_kernel(own_ref, other_ref, halo_ref, *outs):
    for i, ref in enumerate(outs):
        total = own_ref[i].astype(jnp.float32) + other_ref[i].astype(jnp.float32) + halo_ref[i].astype(jnp.float32)
        ref[...] = total.astype(BF16)


def total(own, other, halo):
    _, _, rows, width = own.shape
    return pl.pallas_call(
        total_kernel,
        in_specs=[NEAR] * 3,
        out_specs=[NEAR] * 4,
        out_shape=[jax.ShapeDtypeStruct((2, rows, width), BF16)] * 4,
        compiler_params=limit(12),
        cost_estimate=pl.CostEstimate(flops=own.size * 2, bytes_accessed=own.size * 8, transcendentals=0),
    )(own, other, halo)


def bias_kernel(rows, ids_ref, bias_ref):
    tiles, entries = ids_ref.shape
    rings = lax.axis_size("row")
    core, pair, row = lax.axis_index("core"), lax.axis_index("pair"), lax.axis_index("row")
    first = (lax.axis_index("group") * 2 + core - 1) * tiles
    near = jnp.where(core == 0, 2 * tiles, 0)
    blocks = [lax.rem(row - b + rings, rings) * 2 + (pair ^ a) for a, b in SHIFTS]
    token = lax.broadcasted_iota(jnp.int32, (1, rows), 1)
    own = jnp.concatenate([(token + block * rows) // TILE for block in blocks], axis=1)
    columns = jnp.concatenate([own + tiles, own + near, own + 2 * tiles - near], axis=1) + first
    lists = []
    for t in range(tiles):
        listed = columns < 0
        for n in range(entries):
            key = ids_ref[t, n]
            listed = listed | (columns == jnp.where(key >= 0, key, -7 * tiles))
        lists.append(jnp.where(listed & (columns >= 0), 0.0, MASKED))
    token = lax.broadcasted_iota(jnp.int32, (rows, 1), 0)
    for i, block in enumerate(blocks):
        tile = (token + block * rows) // TILE
        bias = jnp.broadcast_to(lists[0], (rows, columns.shape[1]))
        for t in range(1, tiles):
            bias = jnp.where(tile == t, lists[t], bias)
        bias_ref[i * rows : (i + 1) * rows] = bias


def slab_ids(neighbours):
    rings = lax.axis_size("row")
    swap = []
    for p in range(2):
        for r in range(rings):
            for c in range(2):
                swap.append(((p * rings + r) * 2 + c, (c * rings + r) * 2 + p))
    return lax.ppermute(neighbours, PLANE, swap)


def window_bias(ids, rows):
    slab = 4 * rows
    return pl.pallas_call(
        functools.partial(bias_kernel, rows),
        in_specs=[pl.BlockSpec(memory_space=pltpu.SMEM)],
        out_specs=pl.BlockSpec(memory_space=pltpu.VMEM),
        out_shape=jax.ShapeDtypeStruct((slab, 3 * slab), jnp.float32),
        compiler_params=limit(8),
        cost_estimate=pl.CostEstimate(flops=20 * slab * slab, bytes_accessed=12 * slab * slab, transcendentals=0),
    )(ids)


def per_device(query_in, key_in, value_in, grad_out, neighbours):
    groups, rings = lax.axis_size("group"), lax.axis_size("row")
    rows, full_width = query_in.shape
    group_width = full_width // (2 * rings)

    def place(g, p, r, c):
        return ((g * 2 + p) * rings + r) * 2 + c

    everyone = [(g, p, r, c) for g in range(groups) for p in range(2) for r in range(rings) for c in range(2)]

    def spread_pairs(shift):
        a, b = shift
        return [(place(g, p, r, c), place(g, c ^ a, (r + b) % rings, p)) for g, p, r, c in everyone]

    beside = []
    for g, p, r, c in everyone:
        to = g + 1 if c == 1 else g - 1
        inside = 0 <= to < groups
        beside.append((place(g, p, r, c), place(to, p, r, 1 - c) if inside else place(g, p, r, c)))

    def send(messages):
        return [lax.ppermute(m, AXES, spread_pairs(s)) for m, s in zip(messages, SHIFTS)]

    def send_back(messages, order=(0, 1, 2, 3)):
        back = dict.fromkeys(range(4))
        for i in order:
            back[i] = lax.ppermute(messages[i], AXES, [(d, s) for s, d in spread_pairs(SHIFTS[i])])
        return list(back.values())

    def across(x):
        return lax.ppermute(x, "core", [(0, 1), (1, 0)])

    def halo(x):
        return lax.ppermute(x, AXES, beside)

    key_out = pack(key_in, value_in, group_width)
    key_out, query_in, neighbours = lax.optimization_barrier((key_out, query_in, neighbours))
    query_out = list(pack(query_in, grad_out, group_width))
    owns, ids = lax.optimization_barrier((send(key_out), slab_ids(neighbours)))
    own = join(owns)
    query_out[EARLY:], own = lax.optimization_barrier((query_out[EARLY:], own))
    other = across(own)
    query_out[3], other = lax.optimization_barrier((query_out[3], other))
    far = halo(own)
    queries = send(query_out)
    bias = window_bias(ids, rows)
    oq, own_part, other_part, far_part = attend(bias, queries, own, other, far)
    other_part = across(other_part)
    other_part, oq[3] = lax.optimization_barrier((other_part, oq[3]))
    grads = total(own_part, other_part, halo(far_part))
    forward = unpack(send_back(oq, BACK), full_width, BACK)
    return *forward, *unpack(send_back(grads, BACK), full_width, BACK)


def solution(mesh):
    slabs, heads = mesh.devices.shape
    paired = Mesh(mesh.devices.reshape(slabs // 2, 2, heads // 2, 2), AXES)
    tokens = P(AXES, None)
    return jax.shard_map(
        per_device,
        mesh=paired,
        in_specs=(tokens, tokens, tokens, tokens, P(("group", "pair"), None)),
        out_specs=(tokens, tokens, tokens, tokens),
        check_vma=False,
    )
```
